128 devices in a mesh: dp: 4 (over z), seq: 32 (over x, y, core).
Axes of the slice: x: 4, y: 4, z: 4, core: 2. Of those that a mesh axis runs over, the one named last changes fastest.
Arguments:
- tokens: bfloat16 [8192, 4096], P(('dp', 'seq')), may hold values from -240 to 240
- grad_in: bfloat16 [8192, 4096], P(('dp', 'seq')), may hold values from -6 to 6
- enc_store: bfloat16 [512, 128, 896], P(('dp', 'seq')), may hold values from -6 to 6
- nbr_owner: int32 [4, 64], replicated, may hold values from 0 to 3
- nbr_row: int32 [4, 64], replicated, may hold values from 0 to 3
- w_query: bfloat16 [4096, 4096], P(None, 'seq'), may hold values from -0.09375 to 0.09375
- w_key: bfloat16 [896, 4096], P(None, 'seq'), may hold values from -0.1875 to 0.1875
- w_value: bfloat16 [896, 4096], P(None, 'seq'), may hold values from -0.1875 to 0.1875
- w_out: bfloat16 [4096, 4096], P('seq'), may hold values from -0.09375 to 0.09375
Outputs:
- grad_tokens: bfloat16 [8192, 4096], P(('dp', 'seq'))
- grad_query: float32 [4096, 4096], P(None, 'seq')
- grad_key: float32 [896, 4096], P(None, 'seq')
- grad_value: float32 [896, 4096], P(None, 'seq')
- grad_out: float32 [4096, 4096], P('seq')
The draws below stay inside these ranges and needn't reach their ends.
All inputs are finite; a program needn't handle non-finite values.
Results may differ from the reference program's by a relative error of at most 0.023.
The reference program's roundings to bfloat16 on the way count: a program that leaves them out, or rounds other values in their place, can miss the bound.
Values may be sent and summed in bfloat16 or wider, within the bound.
No kernel may reach another device: no remote copies, remote signals or barrier semaphores. Data moves between devices by JAX's collectives and lax.ppermute only.
A program may use at most 192 MiB of HBM per device.

```python
import math
import jax
import jax.numpy as jnp
import numpy as np
from jax import lax

D = 4096
DH = 128
ENC = 896
STRETCH = 64
NBRS = 2
NBR_LEN = 128
HEAD_DEV = 1
SLOT_DEV = 2
HEADS = 32
HD = 4096
TOKENS = 2048
STRETCHES = 32
SLOTS = 64
STORE_DEV = 4
BATCH_TOK = 8192
STORE_ALL = 512
N_DP = 4
N_SEQ = 32


def draw_tokens(key, part):
    key = jax.random.fold_in(key, 11)
    key_vals, key_scale = jax.random.split(key)
    entries = jnp.clip(jax.random.normal(key_vals, (N_DP * TOKENS, D), jnp.float32), -6.0, 6.0)
    top_log = math.log(8.0)
    row_scale = jnp.exp(jax.random.uniform(key_scale, (N_DP * TOKENS, 1), jnp.float32, 0.0, top_log))
    return (entries * row_scale).astype(jnp.bfloat16)


def with_ends(drawn, rng, smallest, high):
    longest = drawn.shape.index(max(drawn.shape))
    spots = []
    for shift in (0, 1):
        where = [jax.random.randint(jax.random.fold_in(rng, axis), (), 0, length) for axis, length in enumerate(drawn.shape)]
        where[longest] = (where[longest] + shift) % drawn.shape[longest]
        spots.append(tuple(where))
    return drawn.at[spots[0]].set(smallest).at[spots[1]].set(high)


def level_of(key, shape, cuts, least, high):
    def one(dim, blocks):
        draws = jax.random.uniform(jax.random.fold_in(jax.random.fold_in(key, 6), dim), (blocks,), jnp.float32, least / len(cuts), high / len(cuts))
        return jnp.repeat(jnp.exp(draws), shape[dim] // blocks).reshape((-1,) + (1,) * (len(shape) - dim - 1))

    level = one(*cuts[0])
    for cut in cuts[1:]:
        level = level * one(*cut)
    return level


def rank_table(amount, skew):
    weights = [(1 << 20) // math.isqrt(grade ** skew) + 1 for grade in range(1, amount + 1)]
    width = 1 + sum(weights) // (1 << 30)
    return np.cumsum(np.array([max(1, weight // width) for weight in weights]))


def ranked_ids(stream_key, shape, number_of, skew):
    listing = rank_table(number_of, skew)
    ticket = jax.random.randint(jax.random.fold_in(stream_key, 1), shape, 0, int(listing[number_of - 1]))
    standing = jnp.searchsorted(jnp.asarray(listing, jnp.int32), ticket, side="right")
    return jax.random.permutation(jax.random.fold_in(stream_key, 2), number_of)[standing].astype(jnp.int32)


def centred(key, dims, scale, bound, cuts=(), held_as=jnp.bfloat16):
    result = jax.random.normal(key, dims, jnp.float32) * scale
    if len(cuts) > 0:
        result = level_of(key, dims, cuts, -0.22, 0.18) * result
    return jnp.clip(result, min=-bound, max=bound).astype(held_as)


def setup_inputs(seed: int = 0) -> dict:
    key_list = jax.random.split(jax.random.key(seed), 10)
    return {
        "tokens": draw_tokens(jax.random.fold_in(key_list[9], 71), 0),
        "grad_in": centred(key_list[1], (BATCH_TOK, D), 1.0, 6.0, ((0, 128),)),
        "enc_store": centred(key_list[2], (STORE_ALL, NBR_LEN, ENC), 1.0, 6.0, ((0, 128),)),
        "nbr_owner": with_ends(ranked_ids(key_list[3], (N_DP, SLOTS), N_DP, 2), jax.random.fold_in(key_list[3], 3), 0, N_DP - 1).astype(jnp.int32),
        "nbr_row": with_ends(jax.random.randint(key_list[4], (N_DP, SLOTS), 0, STORE_DEV), jax.random.fold_in(key_list[4], 1), 0, STORE_DEV - 1).astype(jnp.int32),
        "w_query": centred(key_list[5], (D, HD), D ** -0.5, 0.09375, ((1, 32),)),
        "w_key": centred(key_list[6], (ENC, HD), ENC ** -0.5, 0.1875, ((1, 32),)),
        "w_value": centred(key_list[7], (ENC, HD), ENC ** -0.5, 0.1875, ((1, 32),)),
        "w_out": centred(key_list[8], (HD, D), HD ** -0.5, 0.09375, ((0, 32),)),
    }


def shift_rows(array_in, margin):
    filler = jnp.zeros((margin,) + array_in.shape[1:], array_in.dtype)
    return jnp.concatenate([array_in[margin:], filler], 0)

def unshift_rows(array_in, margin):
    filler = jnp.zeros((margin,) + array_in.shape[1:], array_in.dtype)
    return jnp.concatenate([filler, array_in[:array_in.shape[0] - margin]], 0)

def inner(left, right):
    return lax.dot_general(left, right, (((0,), (0,)), ((), ())), preferred_element_type=jnp.float32)

def reference(tokens, grad_in, enc_store, nbr_owner, nbr_row, w_query, w_key, w_value, w_out):
    head_cols = HEADS * DH
    key_span = NBRS * NBR_LEN
    inv_root = 1.0 / math.sqrt(DH)
    margin = STRETCH - 1
    grad_query = jnp.zeros((D, head_cols), jnp.float32)
    grad_key = jnp.zeros((ENC, head_cols), jnp.float32)
    grad_value = jnp.zeros((ENC, head_cols), jnp.float32)
    grad_out = jnp.zeros((head_cols, D), jnp.float32)
    token_parts = []
    for index_dp in range(N_DP):
        tok_group = tokens[index_dp * TOKENS:(index_dp + 1) * TOKENS]
        cot_group = grad_in[index_dp * TOKENS:(index_dp + 1) * TOKENS]
        slot_ids = jnp.arange(SLOTS, dtype=jnp.int32)
        store_ids = ((nbr_owner[index_dp] * N_SEQ + slot_ids // SLOT_DEV) * STORE_DEV + nbr_row[index_dp]).astype(jnp.int32)
        neighbours = jnp.take(enc_store, store_ids, axis=0).reshape(SLOTS * NBR_LEN, ENC)
        query_rows = jnp.dot(tok_group, w_query, preferred_element_type=jnp.float32).astype(jnp.bfloat16)
        key_rows = jnp.dot(neighbours, w_key, preferred_element_type=jnp.float32).astype(jnp.bfloat16)
        value_rows = jnp.dot(neighbours, w_value, preferred_element_type=jnp.float32).astype(jnp.bfloat16)
        q_blocks = shift_rows(query_rows, margin).reshape(STRETCHES, STRETCH, HEADS, DH).astype(jnp.float32)
        k_blocks = key_rows.reshape(STRETCHES, key_span, HEADS, DH).astype(jnp.float32)
        v_blocks = value_rows.reshape(STRETCHES, key_span, HEADS, DH).astype(jnp.float32)
        scores = jnp.einsum('cqhd,ckhd->chqk', q_blocks, k_blocks) * inv_root
        attn_probs = jax.nn.softmax(scores, axis=-1)
        probs_low = lax.optimization_barrier(attn_probs.astype(jnp.bfloat16)).astype(jnp.float32)
        context = jnp.einsum('chqk,ckhd->cqhd', probs_low, v_blocks).astype(jnp.bfloat16)
        context = unshift_rows(context.reshape(TOKENS, head_cols), margin)
        grad_out = grad_out + inner(context, cot_group)
        grad_context = lax.dot_general(cot_group, w_out, (((1,), (1,)), ((), ())), preferred_element_type=jnp.float32).astype(jnp.bfloat16)
        grad_blocks = shift_rows(grad_context, margin).reshape(STRETCHES, STRETCH, HEADS, DH).astype(jnp.float32)
        grad_probs = jnp.einsum('cqhd,ckhd->chqk', grad_blocks, v_blocks)
        grad_value_rows = jnp.einsum('chqk,cqhd->ckhd', probs_low, grad_blocks).astype(jnp.bfloat16)
        row_dot = lax.optimization_barrier(jnp.sum(grad_probs * attn_probs, axis=-1, keepdims=True))
        grad_scores = (attn_probs * (grad_probs - row_dot) * inv_root).astype(jnp.bfloat16)
        grad_scores = lax.optimization_barrier(grad_scores).astype(jnp.float32)
        grad_query_rows = jnp.einsum('chqk,ckhd->cqhd', grad_scores, k_blocks).astype(jnp.bfloat16)
        grad_query_rows = unshift_rows(grad_query_rows.reshape(TOKENS, head_cols), margin)
        grad_key_rows = jnp.einsum('chqk,cqhd->ckhd', grad_scores, q_blocks).astype(jnp.bfloat16)
        grad_query = grad_query + inner(tok_group, grad_query_rows)
        grad_key = grad_key + inner(neighbours, grad_key_rows.reshape(SLOTS * NBR_LEN, head_cols))
        grad_value = grad_value + inner(neighbours, grad_value_rows.reshape(SLOTS * NBR_LEN, head_cols))
        term_sum = jnp.zeros((TOKENS, D), jnp.float32)
        block_cols = HEAD_DEV * DH
        for index_seq in range(N_SEQ):
            low = index_seq * block_cols
            term = lax.dot_general(grad_query_rows[:, low:low + block_cols], w_query[:, low:low + block_cols], (((1,), (1,)), ((), ())), preferred_element_type=jnp.float32)
            term_sum = term_sum + lax.optimization_barrier(term.astype(jnp.bfloat16)).astype(jnp.float32)
        token_parts.append(term_sum.astype(jnp.bfloat16))
    grad_tokens = jnp.concatenate(token_parts, 0)
    return (grad_tokens, grad_query, grad_key, grad_value, grad_out)
```

```python
import math

import jax
import jax.numpy as jnp
from jax import lax
from jax.experimental import pallas as pl
from jax.experimental.pallas import tpu as pltpu
from jax.sharding import Mesh, PartitionSpec as P

DH = 128
ENC = 896
STRETCH = 64
NBRS = 2
NBR_LEN = 128
SPAN = NBRS * NBR_LEN
HEADS = 4
EARLY, LATE = (2, 1), (3, 0)
BF = jnp.bfloat16
ROWS = ("x", "c")
SEQ = ("x", "y", "c")


def dot(left, right, dims):
    return lax.dot_general(left, right, (dims, ((), ())), preferred_element_type=jnp.float32)


def forward_kernel(place_ref, q_ref, n_ref, *refs):
    w_refs, (kv_ref, probs_ref, ctx_ref) = refs[:HEADS], refs[-3:]
    heads = range(HEADS)
    inv_root = 1.0 / math.sqrt(DH)
    n = n_ref[...]
    kv = [dot(n, w_refs[h][...], ((1,), (0,))).astype(BF) for h in heads]
    scores = [
        dot(q_ref[:, h * DH : (h + 1) * DH], kv[h][:, :DH], ((1,), (1,))) * inv_root for h in heads
    ]
    weights = [jnp.exp(s - jnp.max(s, axis=-1, keepdims=True)) for s in scores]
    probs = [w / jnp.sum(w, axis=-1, keepdims=True) for w in weights]
    ctx = [dot(probs[h].astype(BF), kv[h][:, DH:], ((1,), (0,))).astype(BF) for h in heads]
    for h in heads:
        kv_ref[:, 2 * h * DH : 2 * (h + 1) * DH] = kv[h]
        probs_ref[0, h] = probs[h]
        place = lax.rem(place_ref[0] + h, HEADS) * DH
        ctx_ref[:, pl.ds(pl.multiple_of(place, DH), DH)] = ctx[h]


def backward_kernel(place_ref, q_ref, g_ref, kv_ref, probs_ref, dq_ref, early_ref, late_ref, dkv_ref):
    heads = range(HEADS)
    inv_root = 1.0 / math.sqrt(DH)
    q = [q_ref[:, h * DH : (h + 1) * DH] for h in heads]
    g = [g_ref[:, h * DH : (h + 1) * DH] for h in heads]
    k = [kv_ref[:, 2 * h * DH : (2 * h + 1) * DH] for h in heads]
    v = [kv_ref[:, (2 * h + 1) * DH : 2 * (h + 1) * DH] for h in heads]
    probs = [probs_ref[0, h] for h in heads]
    grad_probs = [dot(g[h], v[h], ((1,), (1,))) for h in heads]
    row_dot = [jnp.sum(grad_probs[h] * probs[h], axis=-1, keepdims=True) for h in heads]
    grad_scores = [
        (probs[h] * (grad_probs[h] - row_dot[h]) * inv_root).astype(BF) for h in heads
    ]
    dv = [dot(probs[h].astype(BF), g[h], ((0,), (0,))).astype(BF) for h in heads]
    dq = [dot(grad_scores[h], k[h], ((1,), (0,))).astype(BF) for h in heads]
    dk = [dot(grad_scores[h], q[h], ((0,), (0,))).astype(BF) for h in heads]
    for h in heads:
        dq_ref[:, h * DH : (h + 1) * DH] = dq[h]
        place = pl.multiple_of(lax.rem(place_ref[0] + h, HEADS) * DH, DH)
        dkv_ref[:, pl.ds(pl.multiple_of(2 * place, DH), DH)] = dk[h]
        dkv_ref[:, pl.ds(pl.multiple_of(2 * place + DH, DH), DH)] = dv[h]
    for i in range(2):
        early_ref[:, i * DH : (i + 1) * DH] = dq[EARLY[i]]
        late_ref[:, i * DH : (i + 1) * DH] = dq[LATE[i]]


def over_stretches(kernel, operands, others, out_shapes, flops, transcendentals=0):
    others = jax.tree.leaves(others)
    count = operands[0].shape[0] // STRETCH

    def spec(array):
        block = (array.shape[0] // count,) + array.shape[1:]
        return pl.BlockSpec(block, lambda i, _: (i,) + (0,) * (len(block) - 1))

    flat, specs = [], []
    for operand in operands:
        if isinstance(operand, list):
            flat += operand
            specs += [pl.BlockSpec(array.shape, lambda i, _: (0, 0)) for array in operand]
        else:
            flat.append(operand)
            specs.append(spec(operand))
    arrays = flat + out_shapes
    return pl.pallas_call(
        kernel,
        grid_spec=pltpu.PrefetchScalarGridSpec(
            num_scalar_prefetch=1,
            grid=(count,),
            in_specs=specs + [pl.BlockSpec(memory_space=pl.ANY)] * len(others),
            out_specs=[spec(array) for array in out_shapes],
        ),
        out_shape=out_shapes,
        compiler_params=pltpu.CompilerParams(vmem_limit_bytes=40 * 1024 * 1024),
        cost_estimate=pl.CostEstimate(
            flops=flops,
            bytes_accessed=sum(array.size * array.dtype.itemsize for array in arrays),
            transcendentals=transcendentals,
        ),
    )(lax.axis_index("y").reshape(1), *flat, *others)


def forward(q, n_rows, w_pairs, *others):
    rows, cols = q.shape
    out_shapes = [
        jax.ShapeDtypeStruct((n_rows.shape[0], 2 * cols), BF),
        jax.ShapeDtypeStruct((rows // STRETCH, HEADS, STRETCH, SPAN), jnp.float32),
        jax.ShapeDtypeStruct(q.shape, BF),
    ]
    flops = 4 * rows * SPAN * cols + 4 * n_rows.size * cols
    return over_stretches(
        forward_kernel, [q, n_rows, w_pairs], others, out_shapes, flops, rows * SPAN * HEADS
    )


def backward(q, g, kv, probs):
    out_shapes = [
        jax.ShapeDtypeStruct(q.shape, BF),
        jax.ShapeDtypeStruct((q.shape[0], 2 * DH), BF),
        jax.ShapeDtypeStruct((q.shape[0], 2 * DH), BF),
        jax.ShapeDtypeStruct(kv.shape, BF),
    ]
    flops = 8 * q.shape[0] * SPAN * q.shape[1]
    return over_stretches(backward_kernel, [q, g, kv, probs], [], out_shapes, flops)


def hop(array, axis, step):
    n = lax.axis_size(axis)
    return lax.ppermute(array, axis, [(i, (i + step) % n) for i in range(n)])


def idle_kernel(*refs):
    del refs


def after(arrays, *others):
    flat, tree = jax.tree.flatten(arrays)
    operands = flat + jax.tree.leaves(others)
    anywhere = pl.BlockSpec(memory_space=pl.ANY)
    kept = pl.pallas_call(
        idle_kernel,
        in_specs=[anywhere] * len(operands),
        out_specs=[anywhere] * len(flat),
        out_shape=[jax.ShapeDtypeStruct(array.shape, array.dtype) for array in flat],
        input_output_aliases={i: i for i in range(len(flat))},
        cost_estimate=pl.CostEstimate(flops=0, bytes_accessed=0, transcendentals=0),
    )(*operands)
    return jax.tree.unflatten(tree, kept)


def near(block, axis):
    return hop(block, axis, -1), hop(block, axis, 1)


def far(later, before, axis):
    half = later.shape[0] // 2
    return jnp.concatenate([hop(later[:half], axis, -1), hop(before[half:], axis, 1)], 0)


def gather_ring(block, axis):
    later, before = near(block, axis)
    return [block, later, far(later, before, axis), before]


def reduce_ring(parts, axis):
    own, later, opposite, before = parts
    half = opposite.shape[0] // 2
    low = hop(opposite[:half], axis, 1)
    high = hop(opposite[half:], axis, -1)
    later = jnp.concatenate([later[:half] + low, later[half:]], 0)
    before = jnp.concatenate([before[:half], before[half:] + high], 0)
    f32 = jnp.float32
    total = own.astype(f32) + hop(later, axis, 1).astype(f32) + hop(before, axis, -1).astype(f32)
    return total.astype(BF)


def sum_kernel(in_ref, *out_refs):
    total = jnp.sum(in_ref[...].astype(jnp.float32), 0).astype(BF)
    for i in range(2):
        out_refs[i][...] = total[:, i * DH : (i + 1) * DH]


def sum_pair(array):
    n = lax.axis_size("z")
    terms = lax.all_to_all(array, "z", split_axis=0, concat_axis=0, tiled=True)
    rows, cols = array.shape[0] // n, array.shape[1]
    size = rows // 4
    return pl.pallas_call(
        sum_kernel,
        grid=(4,),
        in_specs=[pl.BlockSpec((n, size, cols), lambda i: (0, i, 0))],
        out_specs=[pl.BlockSpec((size, DH), lambda i: (i, 0))] * 2,
        out_shape=[jax.ShapeDtypeStruct((rows, DH), BF)] * 2,
        cost_estimate=pl.CostEstimate(
            flops=array.size, bytes_accessed=2 * array.size, transcendentals=0
        ),
    )(terms.reshape(n, rows, cols))


def sum_parts(array, axis):
    terms = lax.all_to_all(array, axis, split_axis=0, concat_axis=0, tiled=True)
    terms = terms.reshape((lax.axis_size(axis), -1) + array.shape[1:]).astype(jnp.float32)
    return jnp.sum(terms, 0).astype(BF)


def z_gather(block):
    n = lax.axis_size("z")
    blocks = gather_ring(block, "z")
    size = block.shape[0]
    start = lax.rem(n - lax.axis_index("z"), n) * size
    twice = jnp.concatenate(blocks + blocks[:-1], 0)
    return lax.dynamic_slice_in_dim(twice, start, n * size, 0).astype(jnp.float32)


def z_spread(block):
    n = lax.axis_size("z")
    copies = jnp.broadcast_to(block[None], (n,) + block.shape).reshape((-1,) + block.shape[1:])
    blocks = lax.all_to_all(copies, "z", split_axis=0, concat_axis=0, tiled=True)
    return blocks.astype(jnp.float32)


def shift(block):
    n = lax.axis_size(SEQ)
    later = lax.ppermute(block, SEQ, [(i, i - 1) for i in range(1, n)])
    return jnp.concatenate([block[STRETCH - 1 :], later[: STRETCH - 1]], 0)


def unshift(block):
    n = lax.axis_size(SEQ)
    earlier = lax.ppermute(block, SEQ, [(i, i + 1) for i in range(n - 1)])
    return jnp.concatenate([earlier[1:], block[:1]], 0)


def copy_kernel(ids_ref, in_ref, *refs):
    refs[-1][...] = in_ref[...]


def pick(units, ids, *others):
    others = jax.tree.leaves(others)
    block = (1,) + units.shape[1:]
    return pl.pallas_call(
        copy_kernel,
        grid_spec=pltpu.PrefetchScalarGridSpec(
            num_scalar_prefetch=1,
            grid=ids.shape,
            in_specs=[pl.BlockSpec(block, lambda i, ids_ref: (ids_ref[i], 0, 0))]
            + [pl.BlockSpec(memory_space=pl.ANY)] * len(others),
            out_specs=pl.BlockSpec(block, lambda i, ids_ref: (i, 0, 0)),
        ),
        out_shape=jax.ShapeDtypeStruct(ids.shape + units.shape[1:], units.dtype),
        cost_estimate=pl.CostEstimate(
            flops=0, bytes_accessed=4 * ids.size * units[0].size, transcendentals=0
        ),
    )(ids, units, *others)


def shards(tokens, grad_in, enc_store, nbr_owner, nbr_row, w_query, w_key, w_value, w_out):
    w_pair = jnp.concatenate([w_key, w_value], 1)
    first = lax.axis_index(SEQ) * NBRS
    owners = lax.dynamic_slice_in_dim(nbr_owner, first, NBRS, 1)
    rows = lax.dynamic_slice_in_dim(nbr_row, first, NBRS, 1)
    own = lax.dynamic_index_in_dim(owners, lax.axis_index("z"), 0, keepdims=False)
    from_units = own * NBRS + jnp.arange(NBRS, dtype=jnp.int32)

    t_own = shift(tokens)
    q_near = near(w_query, "y")
    t_rows = lax.all_gather(t_own, ROWS, axis=0, tiled=True)
    g_own = shift(grad_in)
    outgoing = pick(enc_store, rows.reshape(-1), t_own)
    arrived = lax.all_to_all(outgoing, "z", split_axis=0, concat_axis=0, tiled=True)
    units = pick(arrived, from_units, t_rows, q_near, g_own)
    n_rows = lax.all_gather(units, ROWS, axis=0, tiled=True).reshape(-1, ENC)
    pair_near = near(w_pair, "y")
    q_far = far(*q_near, "y")
    pair_far = far(*pair_near, "y")
    out_near = near(after(w_out, q_near), "y")
    g_own = after(g_own, n_rows, q_far, out_near)
    g_rows = lax.all_gather(g_own, ROWS, axis=0, tiled=True)
    wq = jnp.concatenate([w_query, q_near[0], q_far, q_near[1]], 1)
    q = dot(t_rows, wq, ((1,), (0,))).astype(BF)
    w_pairs = [w_pair, pair_near[0], pair_far, pair_near[1]]
    kv, probs, ctx = forward(q, n_rows, w_pairs)
    half = w_out.shape[0] // 2
    out_far = [hop(out_near[0][:half], "y", -1), hop(out_near[1][half:], "y", 1)]
    d_out = dot(after(ctx, out_far), g_rows, ((0,), (0,))).astype(BF)
    wo = jnp.concatenate([w_out, out_near[0], *out_far, out_near[1]], 0)
    g = dot(g_rows, after(wo, d_out), ((1,), (1,))).astype(BF)
    dq, early, late, dkv = backward(q, g, kv, probs)
    early = dot(t_rows, early, ((0,), (0,))).astype(BF)
    term = dot(after(dq, early), wq, ((1,), (1,))).astype(BF)
    d_pair = dot(after(dkv, term), n_rows, ((0,), (0,))).astype(BF)
    early = sum_pair(early)
    late = sum_pair(after(dot(t_rows, late, ((0,), (0,))).astype(BF), early, d_pair))

    d_out = lax.psum_scatter(d_out, "y", scatter_dimension=0, tiled=True)
    d_pair = lax.psum_scatter(after(d_pair, d_out, early), "y", scatter_dimension=0, tiled=True)
    late = after(late, d_pair)
    term = lax.psum_scatter(after(term, d_pair), ROWS, scatter_dimension=0, tiled=True)
    d_query = reduce_ring([late[1], early[1], early[0], late[0]], "y")
    width = d_out.shape[1]
    d_pair = d_pair.reshape(4, -1, 2, ENC)
    rest = jnp.concatenate([d_out.reshape(4, -1, width), d_pair[:, :, 0], d_pair[:, :, 1]], 2)
    rest = sum_parts(after(rest, late).reshape(DH, -1), "z")
    d_query = z_gather(after(d_query, rest))
    rest = z_gather(rest)
    d_out = rest[:, :width]
    d_pair = jnp.stack([rest[:, width : width + ENC], rest[:, width + ENC :]], 1)
    d_pair = d_pair.reshape(2 * DH, ENC).T
    grad_tokens = unshift(term)
    return grad_tokens, d_query, d_pair[:, :DH], d_pair[:, DH:], d_out


def solution(mesh):
    devices = mesh.devices.reshape(4, 4, 4, 2)
    torus = Mesh(devices, ("z", "x", "y", "c"))
    rows = P(("z", "x", "y", "c"))
    cols = P(None, SEQ)
    in_specs = (rows, rows, rows, P(), P(), cols, cols, cols, P(SEQ))
    out_specs = (rows, cols, cols, cols, P(SEQ))
    return jax.shard_map(shards, mesh=torus, in_specs=in_specs, out_specs=out_specs, check_vma=False)
```

```python
import functools
import math

import jax
import jax.numpy as jnp
from jax import lax
from jax.experimental import pallas as pl
from jax.experimental.pallas import tpu as pltpu
from jax.sharding import Mesh, PartitionSpec as P

DH = 128
ENC = 896
STRETCH = 64
NBRS = 2
NBR_LEN = 128
SPAN = NBRS * NBR_LEN
HEADS = 4
EARLY, LATE = (2, 1), (3, 0)
BF = jnp.bfloat16
PARTS = 4
ANYWHERE = pl.BlockSpec(memory_space=pl.ANY)
PARAMS = pltpu.CompilerParams(vmem_limit_bytes=40 * 1024 * 1024)
ROWS = ("x", "c")
SEQ = ("x", "y", "c")


def dot(left, right, dims):
    return lax.dot_general(left, right, (dims, ((), ())), preferred_element_type=jnp.float32)


def forward_kernel(place_ref, q_ref, n_ref, *refs):
    w_refs, (kv_ref, probs_ref, ctx_ref) = refs[:HEADS], refs[-3:]
    heads = range(HEADS)
    inv_root = 1.0 / math.sqrt(DH)
    n = n_ref[...]
    pairs = [jnp.concatenate([w_ref[:ENC], w_ref[ENC:]], 1) for w_ref in w_refs]
    kv = [dot(n, pairs[h], ((1,), (0,))).astype(BF) for h in heads]
    scores = [
        dot(q_ref[:, h * DH : (h + 1) * DH], kv[h][:, :DH], ((1,), (1,))) * inv_root for h in heads
    ]
    weights = [jnp.exp(s - jnp.max(s, axis=-1, keepdims=True)) for s in scores]
    probs = [w / jnp.sum(w, axis=-1, keepdims=True) for w in weights]
    ctx = [dot(probs[h].astype(BF), kv[h][:, DH:], ((1,), (0,))).astype(BF) for h in heads]
    for h in heads:
        kv_ref[:, 2 * h * DH : 2 * (h + 1) * DH] = kv[h]
        probs_ref[0, h] = probs[h]
        place = lax.rem(place_ref[0] + h, HEADS) * DH
        ctx_ref[:, pl.ds(pl.multiple_of(place, DH), DH)] = ctx[h]


def backward_kernel(place_ref, q_ref, g_ref, kv_ref, probs_ref, dq_ref, early_ref, late_ref, dkv_ref):
    heads = range(HEADS)
    inv_root = 1.0 / math.sqrt(DH)
    q = [q_ref[:, h * DH : (h + 1) * DH] for h in heads]
    g = [g_ref[:, h * DH : (h + 1) * DH] for h in heads]
    k = [kv_ref[:, 2 * h * DH : (2 * h + 1) * DH] for h in heads]
    v = [kv_ref[:, (2 * h + 1) * DH : 2 * (h + 1) * DH] for h in heads]
    probs = [probs_ref[0, h] for h in heads]
    grad_probs = [dot(g[h], v[h], ((1,), (1,))) for h in heads]
    row_dot = [jnp.sum(grad_probs[h] * probs[h], axis=-1, keepdims=True) for h in heads]
    grad_scores = [
        (probs[h] * (grad_probs[h] - row_dot[h]) * inv_root).astype(BF) for h in heads
    ]
    dv = [dot(probs[h].astype(BF), g[h], ((0,), (0,))).astype(BF) for h in heads]
    dq = [dot(grad_scores[h], k[h], ((1,), (0,))).astype(BF) for h in heads]
    dk = [dot(grad_scores[h], q[h], ((0,), (0,))).astype(BF) for h in heads]
    for h in heads:
        dq_ref[:, h * DH : (h + 1) * DH] = dq[h]
        place = pl.multiple_of(lax.rem(place_ref[0] + h, HEADS) * DH, DH)
        dkv_ref[:, pl.ds(pl.multiple_of(2 * place, DH), DH)] = dk[h]
        dkv_ref[:, pl.ds(pl.multiple_of(2 * place + DH, DH), DH)] = dv[h]
    for i in range(2):
        early_ref[:, i * DH : (i + 1) * DH] = dq[EARLY[i]]
        late_ref[:, i * DH : (i + 1) * DH] = dq[LATE[i]]


def over_stretches(kernel, operands, others, out_shapes, flops, transcendentals=0):
    others = jax.tree.leaves(others)
    count = operands[0].shape[0] // STRETCH

    def spec(array):
        block = (array.shape[0] // count,) + array.shape[1:]
        return pl.BlockSpec(block, lambda i, _: (i,) + (0,) * (len(block) - 1))

    flat, specs = [], []
    for operand in operands:
        if isinstance(operand, list):
            flat += operand
            specs += [pl.BlockSpec((2 * ENC, DH), lambda i, _: (0, 0)) for array in operand]
        else:
            flat.append(operand)
            specs.append(spec(operand))
    arrays = flat + out_shapes
    return pl.pallas_call(
        kernel,
        grid_spec=pltpu.PrefetchScalarGridSpec(
            num_scalar_prefetch=1,
            grid=(count,),
            in_specs=specs + [pl.BlockSpec(memory_space=pl.ANY)] * len(others),
            out_specs=[spec(array) for array in out_shapes],
        ),
        out_shape=out_shapes,
        compiler_params=PARAMS,
        cost_estimate=pl.CostEstimate(
            flops=flops,
            bytes_accessed=sum(array.size * array.dtype.itemsize for array in arrays),
            transcendentals=transcendentals,
        ),
    )(lax.axis_index("y").reshape(1), *flat, *others)


def forward(q, n_rows, w_ins, *others):
    rows, cols = q.shape
    out_shapes = [
        jax.ShapeDtypeStruct((n_rows.shape[0], 2 * cols), BF),
        jax.ShapeDtypeStruct((rows // STRETCH, HEADS, STRETCH, SPAN), jnp.float32),
        jax.ShapeDtypeStruct(q.shape, BF),
    ]
    flops = 4 * rows * SPAN * cols + 4 * n_rows.size * cols
    return over_stretches(
        forward_kernel, [q, n_rows, w_ins], others, out_shapes, flops, rows * SPAN * HEADS
    )


def backward(q, g, kv, probs):
    out_shapes = [
        jax.ShapeDtypeStruct(q.shape, BF),
        jax.ShapeDtypeStruct((q.shape[0], 2 * DH), BF),
        jax.ShapeDtypeStruct((q.shape[0], 2 * DH), BF),
        jax.ShapeDtypeStruct(kv.shape, BF),
    ]
    flops = 8 * q.shape[0] * SPAN * q.shape[1]
    return over_stretches(backward_kernel, [q, g, kv, probs], [], out_shapes, flops)


def project_kernel(count, a_ref, *refs):
    out_ref, total = refs[-2], refs[-1]
    step = pl.program_id(0)
    w = jnp.concatenate([w_ref[...] for w_ref in refs[:count]], 0)
    term = dot(a_ref[...], w, ((1,), (1,)))

    @pl.when(step == 0)
    def _():
        total[...] = term

    @pl.when(step > 0)
    def _():
        total[...] += term

    @pl.when(step == pl.num_programs(0) - 1)
    def _():
        out_ref[...] = total[...].astype(BF)


def project(array, blocks, *others):
    rows, depth = array.shape
    size = depth // PARTS
    cols = sum(block.shape[0] for block in blocks)
    return pl.pallas_call(
        functools.partial(project_kernel, len(blocks)),
        grid=(PARTS,),
        in_specs=[pl.BlockSpec((rows, size), lambda i: (0, i))]
        + [pl.BlockSpec((block.shape[0], size), lambda i: (0, i)) for block in blocks]
        + [ANYWHERE] * len(others),
        out_specs=pl.BlockSpec((rows, cols), lambda i: (0, 0)),
        out_shape=jax.ShapeDtypeStruct((rows, cols), BF),
        scratch_shapes=[pltpu.VMEM((rows, cols), jnp.float32)],
        compiler_params=pltpu.CompilerParams(vmem_limit_bytes=56 * 1024 * 1024),
        cost_estimate=product_cost(rows, cols, depth),
    )(array, *blocks, *others)


def product_cost(rows, cols, depth):
    return pl.CostEstimate(
        flops=2 * rows * cols * depth,
        bytes_accessed=2 * (rows * cols + rows * depth + cols * depth),
        transcendentals=0,
    )


def hop(array, axis, step):
    n = lax.axis_size(axis)
    return lax.ppermute(array, axis, [(i, (i + step) % n) for i in range(n)])


def idle_kernel(*refs):
    del refs


def after(arrays, *others):
    flat, tree = jax.tree.flatten(arrays)
    operands = flat + jax.tree.leaves(others)
    anywhere = pl.BlockSpec(memory_space=pl.ANY)
    kept = pl.pallas_call(
        idle_kernel,
        in_specs=[anywhere] * len(operands),
        out_specs=[anywhere] * len(flat),
        out_shape=[jax.ShapeDtypeStruct(array.shape, array.dtype) for array in flat],
        input_output_aliases={i: i for i in range(len(flat))},
        cost_estimate=pl.CostEstimate(flops=0, bytes_accessed=0, transcendentals=0),
    )(*operands)
    return jax.tree.unflatten(tree, kept)


def near(block, axis):
    return hop(block, axis, -1), hop(block, axis, 1)


def far(later, before, axis):
    half = later.shape[0] // 2
    return jnp.concatenate([hop(later[:half], axis, -1), hop(before[half:], axis, 1)], 0)


def gather_ring(block, axis):
    later, before = near(block, axis)
    return [block, later, far(later, before, axis), before]


def reduce_ring(parts, axis):
    own, later, opposite, before = parts
    half = opposite.shape[0] // 2
    low = hop(opposite[:half], axis, 1)
    high = hop(opposite[half:], axis, -1)
    later = jnp.concatenate([later[:half] + low, later[half:]], 0)
    before = jnp.concatenate([before[:half], before[half:] + high], 0)
    f32 = jnp.float32
    total = own.astype(f32) + hop(later, axis, 1).astype(f32) + hop(before, axis, -1).astype(f32)
    return total.astype(BF)


def sum_kernel(in_ref, *refs):
    out_refs = refs[-2:]
    total = jnp.sum(in_ref[...].astype(jnp.float32), 0).astype(BF)
    for i in range(2):
        out_refs[i][...] = total[:, i * DH : (i + 1) * DH]


def sum_pair(array, *others):
    n = lax.axis_size("z")
    terms = lax.all_to_all(array, "z", split_axis=0, concat_axis=0, tiled=True)
    rows, cols = array.shape[0] // n, array.shape[1]
    size = rows // 4
    return pl.pallas_call(
        sum_kernel,
        grid=(4,),
        in_specs=[pl.BlockSpec((n, size, cols), lambda i: (0, i, 0))] + [ANYWHERE] * len(others),
        out_specs=[pl.BlockSpec((size, DH), lambda i: (i, 0))] * 2,
        out_shape=[jax.ShapeDtypeStruct((rows, DH), BF)] * 2,
        cost_estimate=pl.CostEstimate(
            flops=array.size, bytes_accessed=2 * array.size, transcendentals=0
        ),
    )(terms.reshape(n, rows, cols), *others)


def sum_parts(array, axis):
    terms = lax.all_to_all(array, axis, split_axis=0, concat_axis=0, tiled=True)
    terms = terms.reshape((lax.axis_size(axis), -1) + array.shape[1:]).astype(jnp.float32)
    return jnp.sum(terms, 0).astype(BF)


def z_gather(block):
    n = lax.axis_size("z")
    blocks = gather_ring(block, "z")
    size = block.shape[0]
    start = lax.rem(n - lax.axis_index("z"), n) * size
    twice = jnp.concatenate(blocks + blocks[:-1], 0)
    return lax.dynamic_slice_in_dim(twice, start, n * size, 0).astype(jnp.float32)


def shift(block):
    n = lax.axis_size(SEQ)
    later = lax.ppermute(block, SEQ, [(i, i - 1) for i in range(1, n)])
    return jnp.concatenate([block[STRETCH - 1 :], later[: STRETCH - 1]], 0)


def unshift(block):
    n = lax.axis_size(SEQ)
    earlier = lax.ppermute(block, SEQ, [(i, i + 1) for i in range(n - 1)])
    return jnp.concatenate([earlier[1:], block[:1]], 0)


def copy_kernel(ids_ref, in_ref, *refs):
    refs[-1][...] = in_ref[...]


def pick(units, ids, *others):
    others = jax.tree.leaves(others)
    block = (1,) + units.shape[1:]
    return pl.pallas_call(
        copy_kernel,
        grid_spec=pltpu.PrefetchScalarGridSpec(
            num_scalar_prefetch=1,
            grid=ids.shape,
            in_specs=[pl.BlockSpec(block, lambda i, ids_ref: (ids_ref[i], 0, 0))]
            + [pl.BlockSpec(memory_space=pl.ANY)] * len(others),
            out_specs=pl.BlockSpec(block, lambda i, ids_ref: (i, 0, 0)),
        ),
        out_shape=jax.ShapeDtypeStruct(ids.shape + units.shape[1:], units.dtype),
        cost_estimate=pl.CostEstimate(
            flops=0, bytes_accessed=4 * ids.size * units[0].size, transcendentals=0
        ),
    )(ids, units, *others)


def shards(tokens, grad_in, enc_store, nbr_owner, nbr_row, w_query, w_key, w_value, w_out):
    w_in = jnp.concatenate([w_key, w_value, w_query], 0)
    first = lax.axis_index(SEQ) * NBRS
    owners = lax.dynamic_slice_in_dim(nbr_owner, first, NBRS, 1)
    rows = lax.dynamic_slice_in_dim(nbr_row, first, NBRS, 1)
    own = lax.dynamic_index_in_dim(owners, lax.axis_index("z"), 0, keepdims=False)
    from_units = own * NBRS + jnp.arange(NBRS, dtype=jnp.int32)

    t_own = shift(tokens)
    in_near = near(w_in, "y")
    t_rows = lax.all_gather(t_own, ROWS, axis=0, tiled=True)
    g_own = shift(grad_in)
    outgoing = pick(enc_store, rows.reshape(-1), t_own)
    arrived = lax.all_to_all(outgoing, "z", split_axis=0, concat_axis=0, tiled=True)
    units = pick(arrived, from_units, t_rows, in_near, g_own)
    n_rows = lax.all_gather(units, ROWS, axis=0, tiled=True).reshape(-1, ENC)
    in_far = far(*in_near, "y")
    out_near = near(after(w_out, in_near), "y")
    g_own = after(g_own, n_rows, in_far)
    g_rows = lax.all_gather(g_own, ROWS, axis=0, tiled=True)
    w_ins = [w_in, in_near[0], in_far, in_near[1]]
    wq = jnp.concatenate([block[2 * ENC :] for block in w_ins], 1)
    q = dot(t_rows, wq, ((1,), (0,))).astype(BF)
    kv, probs, ctx = forward(q, n_rows, w_ins, out_near)
    half = w_out.shape[0] // 2
    out_far = [hop(out_near[0][:half], "y", -1), hop(out_near[1][half:], "y", 1)]
    d_out = dot(after(ctx, out_far), g_rows, ((0,), (0,))).astype(BF)
    g = project(g_rows, [w_out, out_near[0], *out_far, out_near[1]], d_out)
    dq, early, late, dkv = backward(q, g, kv, probs)
    early = dot(t_rows, early, ((0,), (0,))).astype(BF)
    term = dot(after(dq, early), wq, ((1,), (1,))).astype(BF)
    d_pair = dot(after(dkv, term), n_rows, ((0,), (0,))).astype(BF)
    late = dot(t_rows, late, ((0,), (0,))).astype(BF)
    early = sum_pair(early, late)
    late = sum_pair(after(late, early, d_pair))

    d_out = lax.psum_scatter(d_out, "y", scatter_dimension=0, tiled=True)
    d_pair = lax.psum_scatter(after(d_pair, d_out, early), "y", scatter_dimension=0, tiled=True)
    late, term = after((late, term), d_pair)
    term = lax.psum_scatter(term, ROWS, scatter_dimension=0, tiled=True)
    d_query = reduce_ring([late[1], early[1], early[0], late[0]], "y")
    width = d_out.shape[1]
    d_pair = d_pair.reshape(4, -1, 2, ENC)
    rest = jnp.concatenate([d_out.reshape(4, -1, width), d_pair[:, :, 0], d_pair[:, :, 1]], 2)
    rest = sum_parts(after(rest, late).reshape(DH, -1), "z")
    d_query = z_gather(after(d_query, rest))
    rest = z_gather(rest)
    d_out = rest[:, :width]
    d_pair = jnp.stack([rest[:, width : width + ENC], rest[:, width + ENC :]], 1)
    d_pair = d_pair.reshape(2 * DH, ENC).T
    grad_tokens = unshift(term)
    return grad_tokens, d_query, d_pair[:, :DH], d_pair[:, DH:], d_out


def solution(mesh):
    devices = mesh.devices.reshape(4, 4, 4, 2)
    torus = Mesh(devices, ("z", "x", "y", "c"))
    rows = P(("z", "x", "y", "c"))
    cols = P(None, SEQ)
    in_specs = (rows, rows, rows, P(), P(), cols, cols, cols, P(SEQ))
    out_specs = (rows, cols, cols, cols, P(SEQ))
    return jax.shard_map(shards, mesh=torus, in_specs=in_specs, out_specs=out_specs, check_vma=False)
```

```python
import functools
import math

import jax
import jax.numpy as jnp
from jax import lax
from jax.experimental import pallas as pl
from jax.experimental.pallas import tpu as pltpu
from jax.sharding import Mesh, PartitionSpec as P

DH = 128
ENC = 896
STRETCH = 64
NBRS = 2
NBR_LEN = 128
SPAN = NBRS * NBR_LEN
HEADS = 4
EARLY, LATE = (2, 1), (3, 0)
BF = jnp.bfloat16
PARTS = 4
ANYWHERE = pl.BlockSpec(memory_space=pl.ANY)
PARAMS = pltpu.CompilerParams(vmem_limit_bytes=40 * 1024 * 1024)
ROWS = ("x", "c")
SEQ = ("x", "y", "c")


def dot(left, right, dims):
    return lax.dot_general(left, right, (dims, ((), ())), preferred_element_type=jnp.float32)


def forward_kernel(place_ref, q_ref, n_ref, *refs):
    w_refs, (kv_ref, probs_ref, ctx_ref) = refs[:HEADS], refs[-3:]
    heads = range(HEADS)
    inv_root = 1.0 / math.sqrt(DH)
    n = n_ref[...]
    pairs = [jnp.concatenate([w_ref[:ENC], w_ref[ENC:]], 1) for w_ref in w_refs]
    kv = [dot(n, pairs[h], ((1,), (0,))).astype(BF) for h in heads]
    scores = [
        dot(q_ref[:, h * DH : (h + 1) * DH], kv[h][:, :DH], ((1,), (1,))) * inv_root for h in heads
    ]
    weights = [jnp.exp(s - jnp.max(s, axis=-1, keepdims=True)) for s in scores]
    probs = [w / jnp.sum(w, axis=-1, keepdims=True) for w in weights]
    ctx = [dot(probs[h].astype(BF), kv[h][:, DH:], ((1,), (0,))).astype(BF) for h in heads]
    for h in heads:
        kv_ref[:, 2 * h * DH : 2 * (h + 1) * DH] = kv[h]
        probs_ref[0, h] = probs[h]
        place = lax.rem(place_ref[0] + h, HEADS) * DH
        ctx_ref[:, pl.ds(pl.multiple_of(place, DH), DH)] = ctx[h]


def backward_kernel(place_ref, q_ref, g_ref, kv_ref, probs_ref, dq_ref, early_ref, late_ref, dkv_ref):
    heads = range(HEADS)
    inv_root = 1.0 / math.sqrt(DH)
    q = [q_ref[:, h * DH : (h + 1) * DH] for h in heads]
    g = [g_ref[:, h * DH : (h + 1) * DH] for h in heads]
    k = [kv_ref[:, 2 * h * DH : (2 * h + 1) * DH] for h in heads]
    v = [kv_ref[:, (2 * h + 1) * DH : 2 * (h + 1) * DH] for h in heads]
    probs = [probs_ref[0, h] for h in heads]
    grad_probs = [dot(g[h], v[h], ((1,), (1,))) for h in heads]
    row_dot = [jnp.sum(grad_probs[h] * probs[h], axis=-1, keepdims=True) for h in heads]
    grad_scores = [
        (probs[h] * (grad_probs[h] - row_dot[h]) * inv_root).astype(BF) for h in heads
    ]
    dv = [dot(probs[h].astype(BF), g[h], ((0,), (0,))).astype(BF) for h in heads]
    dq = [dot(grad_scores[h], k[h], ((1,), (0,))).astype(BF) for h in heads]
    dk = [dot(grad_scores[h], q[h], ((0,), (0,))).astype(BF) for h in heads]
    for h in heads:
        dq_ref[:, h * DH : (h + 1) * DH] = dq[h]
        place = pl.multiple_of(lax.rem(place_ref[0] + h, HEADS) * DH, DH)
        dkv_ref[:, pl.ds(pl.multiple_of(2 * place, DH), DH)] = dk[h]
        dkv_ref[:, pl.ds(pl.multiple_of(2 * place + DH, DH), DH)] = dv[h]
    for i in range(2):
        early_ref[:, i * DH : (i + 1) * DH] = dq[EARLY[i]]
        late_ref[:, i * DH : (i + 1) * DH] = dq[LATE[i]]


def over_stretches(kernel, operands, others, out_shapes, flops, transcendentals=0):
    others = jax.tree.leaves(others)
    count = operands[0].shape[0] // STRETCH

    def spec(array):
        block = (array.shape[0] // count,) + array.shape[1:]
        return pl.BlockSpec(block, lambda i, _: (i,) + (0,) * (len(block) - 1))

    flat, specs = [], []
    for operand in operands:
        if isinstance(operand, list):
            flat += operand
            specs += [pl.BlockSpec((2 * ENC, DH), lambda i, _: (0, 0)) for array in operand]
        else:
            flat.append(operand)
            specs.append(spec(operand))
    arrays = flat + out_shapes
    return pl.pallas_call(
        kernel,
        grid_spec=pltpu.PrefetchScalarGridSpec(
            num_scalar_prefetch=1,
            grid=(count,),
            in_specs=specs + [pl.BlockSpec(memory_space=pl.ANY)] * len(others),
            out_specs=[spec(array) for array in out_shapes],
        ),
        out_shape=out_shapes,
        compiler_params=PARAMS,
        cost_estimate=pl.CostEstimate(
            flops=flops,
            bytes_accessed=sum(array.size * array.dtype.itemsize for array in arrays),
            transcendentals=transcendentals,
        ),
    )(lax.axis_index("y").reshape(1), *flat, *others)


def forward(q, n_rows, w_ins, *others):
    rows, cols = q.shape
    out_shapes = [
        jax.ShapeDtypeStruct((n_rows.shape[0], 2 * cols), BF),
        jax.ShapeDtypeStruct((rows // STRETCH, HEADS, STRETCH, SPAN), jnp.float32),
        jax.ShapeDtypeStruct(q.shape, BF),
    ]
    flops = 4 * rows * SPAN * cols + 4 * n_rows.size * cols
    return over_stretches(
        forward_kernel, [q, n_rows, w_ins], others, out_shapes, flops, rows * SPAN * HEADS
    )


def backward(q, g, kv, probs):
    out_shapes = [
        jax.ShapeDtypeStruct(q.shape, BF),
        jax.ShapeDtypeStruct((q.shape[0], 2 * DH), BF),
        jax.ShapeDtypeStruct((q.shape[0], 2 * DH), BF),
        jax.ShapeDtypeStruct(kv.shape, BF),
    ]
    flops = 8 * q.shape[0] * SPAN * q.shape[1]
    return over_stretches(backward_kernel, [q, g, kv, probs], [], out_shapes, flops)


def project_kernel(count, a_ref, *refs):
    out_ref, total = refs[-2], refs[-1]
    step = pl.program_id(0)
    w = jnp.concatenate([w_ref[...] for w_ref in refs[:count]], 0)
    term = dot(a_ref[...], w, ((1,), (1,)))

    @pl.when(step == 0)
    def _():
        total[...] = term

    @pl.when(step > 0)
    def _():
        total[...] += term

    @pl.when(step == pl.num_programs(0) - 1)
    def _():
        out_ref[...] = total[...].astype(BF)


def project(array, blocks, *others):
    rows, depth = array.shape
    size = depth // PARTS
    cols = sum(block.shape[0] for block in blocks)
    return pl.pallas_call(
        functools.partial(project_kernel, len(blocks)),
        grid=(PARTS,),
        in_specs=[pl.BlockSpec((rows, size), lambda i: (0, i))]
        + [pl.BlockSpec((block.shape[0], size), lambda i: (0, i)) for block in blocks]
        + [ANYWHERE] * len(others),
        out_specs=pl.BlockSpec((rows, cols), lambda i: (0, 0)),
        out_shape=jax.ShapeDtypeStruct((rows, cols), BF),
        scratch_shapes=[pltpu.VMEM((rows, cols), jnp.float32)],
        compiler_params=pltpu.CompilerParams(vmem_limit_bytes=56 * 1024 * 1024),
        cost_estimate=product_cost(rows, cols, depth),
    )(array, *blocks, *others)


def product_cost(rows, cols, depth):
    return pl.CostEstimate(
        flops=2 * rows * cols * depth,
        bytes_accessed=2 * (rows * cols + rows * depth + cols * depth),
        transcendentals=0,
    )


def hop(array, axis, step):
    n = lax.axis_size(axis)
    return lax.ppermute(array, axis, [(i, (i + step) % n) for i in range(n)])


def idle_kernel(*refs):
    del refs


def after(arrays, *others):
    flat, tree = jax.tree.flatten(arrays)
    operands = flat + jax.tree.leaves(others)
    anywhere = pl.BlockSpec(memory_space=pl.ANY)
    kept = pl.pallas_call(
        idle_kernel,
        in_specs=[anywhere] * len(operands),
        out_specs=[anywhere] * len(flat),
        out_shape=[jax.ShapeDtypeStruct(array.shape, array.dtype) for array in flat],
        input_output_aliases={i: i for i in range(len(flat))},
        cost_estimate=pl.CostEstimate(flops=0, bytes_accessed=0, transcendentals=0),
    )(*operands)
    return jax.tree.unflatten(tree, kept)


def near(block, axis):
    return hop(block, axis, -1), hop(block, axis, 1)


def far(later, before, axis):
    half = later.shape[0] // 2
    return jnp.concatenate([hop(later[:half], axis, -1), hop(before[half:], axis, 1)], 0)


def gather_ring(block, axis):
    later, before = near(block, axis)
    return [block, later, far(later, before, axis), before]


def reduce_ring(parts, axis):
    own, later, opposite, before = parts
    half = opposite.shape[0] // 2
    low = hop(opposite[:half], axis, 1)
    high = hop(opposite[half:], axis, -1)
    later = jnp.concatenate([later[:half] + low, later[half:]], 0)
    before = jnp.concatenate([before[:half], before[half:] + high], 0)
    f32 = jnp.float32
    total = own.astype(f32) + hop(later, axis, 1).astype(f32) + hop(before, axis, -1).astype(f32)
    return total.astype(BF)


def sum_kernel(in_ref, *out_refs):
    total = jnp.sum(in_ref[...].astype(jnp.float32), 0).astype(BF)
    for i in range(2):
        out_refs[i][...] = total[:, i * DH : (i + 1) * DH]


def z_terms(array):
    return lax.all_to_all(array, "z", split_axis=0, concat_axis=0, tiled=True)


def sum_pair(terms):
    n = lax.axis_size("z")
    rows, cols = terms.shape[0] // n, terms.shape[1]
    size = rows // 4
    return pl.pallas_call(
        sum_kernel,
        grid=(4,),
        in_specs=[pl.BlockSpec((n, size, cols), lambda i: (0, i, 0))],
        out_specs=[pl.BlockSpec((size, DH), lambda i: (i, 0))] * 2,
        out_shape=[jax.ShapeDtypeStruct((rows, DH), BF)] * 2,
        cost_estimate=pl.CostEstimate(
            flops=terms.size, bytes_accessed=2 * terms.size, transcendentals=0
        ),
    )(terms.reshape(n, rows, cols))


def sum_parts(array, axis):
    terms = lax.all_to_all(array, axis, split_axis=0, concat_axis=0, tiled=True)
    terms = terms.reshape((lax.axis_size(axis), -1) + array.shape[1:]).astype(jnp.float32)
    return jnp.sum(terms, 0).astype(BF)


def z_gather(block):
    n = lax.axis_size("z")
    blocks = gather_ring(block, "z")
    size = block.shape[0]
    start = lax.rem(n - lax.axis_index("z"), n) * size
    twice = jnp.concatenate(blocks + blocks[:-1], 0)
    return lax.dynamic_slice_in_dim(twice, start, n * size, 0).astype(jnp.float32)


def shift(block):
    n = lax.axis_size(SEQ)
    later = lax.ppermute(block, SEQ, [(i, i - 1) for i in range(1, n)])
    return jnp.concatenate([block[STRETCH - 1 :], later[: STRETCH - 1]], 0)


def unshift(block):
    n = lax.axis_size(SEQ)
    earlier = lax.ppermute(block, SEQ, [(i, i + 1) for i in range(n - 1)])
    return jnp.concatenate([earlier[1:], block[:1]], 0)


def copy_kernel(ids_ref, in_ref, *refs):
    refs[-1][...] = in_ref[...]


def pick(units, ids, *others):
    others = jax.tree.leaves(others)
    block = (1,) + units.shape[1:]
    return pl.pallas_call(
        copy_kernel,
        grid_spec=pltpu.PrefetchScalarGridSpec(
            num_scalar_prefetch=1,
            grid=ids.shape,
            in_specs=[pl.BlockSpec(block, lambda i, ids_ref: (ids_ref[i], 0, 0))]
            + [pl.BlockSpec(memory_space=pl.ANY)] * len(others),
            out_specs=pl.BlockSpec(block, lambda i, ids_ref: (i, 0, 0)),
        ),
        out_shape=jax.ShapeDtypeStruct(ids.shape + units.shape[1:], units.dtype),
        cost_estimate=pl.CostEstimate(
            flops=0, bytes_accessed=4 * ids.size * units[0].size, transcendentals=0
        ),
    )(ids, units, *others)


def shards(tokens, grad_in, enc_store, nbr_owner, nbr_row, w_query, w_key, w_value, w_out):
    w_in = jnp.concatenate([w_key, w_value, w_query], 0)
    first = lax.axis_index(SEQ) * NBRS
    owners = lax.dynamic_slice_in_dim(nbr_owner, first, NBRS, 1)
    rows = lax.dynamic_slice_in_dim(nbr_row, first, NBRS, 1)
    own = lax.dynamic_index_in_dim(owners, lax.axis_index("z"), 0, keepdims=False)
    from_units = own * NBRS + jnp.arange(NBRS, dtype=jnp.int32)

    t_own = shift(tokens)
    in_near = near(w_in, "y")
    t_rows = lax.all_gather(t_own, ROWS, axis=0, tiled=True)
    g_own = shift(grad_in)
    outgoing = pick(enc_store, rows.reshape(-1), t_own)
    arrived = lax.all_to_all(outgoing, "z", split_axis=0, concat_axis=0, tiled=True)
    units = pick(arrived, from_units, t_rows, in_near, g_own)
    n_rows = lax.all_gather(units, ROWS, axis=0, tiled=True).reshape(-1, ENC)
    in_far = far(*in_near, "y")
    out_near = near(after(w_out, in_near), "y")
    g_own = after(g_own, n_rows, in_far)
    g_rows = lax.all_gather(g_own, ROWS, axis=0, tiled=True)
    w_ins = [w_in, in_near[0], in_far, in_near[1]]
    wq = jnp.concatenate([block[2 * ENC :] for block in w_ins], 1)
    q = dot(t_rows, wq, ((1,), (0,))).astype(BF)
    kv, probs, ctx = forward(q, n_rows, w_ins, out_near)
    half = w_out.shape[0] // 2
    out_far = [hop(out_near[0][:half], "y", -1), hop(out_near[1][half:], "y", 1)]
    d_out = dot(after(ctx, out_far), g_rows, ((0,), (0,))).astype(BF)
    g = project(g_rows, [w_out, out_near[0], *out_far, out_near[1]], d_out)
    dq, early, late, dkv = backward(q, g, kv, probs)
    early = dot(t_rows, early, ((0,), (0,))).astype(BF)
    term = dot(after(dq, early), wq, ((1,), (1,))).astype(BF)
    late = dot(t_rows, late, ((0,), (0,))).astype(BF)
    d_pair = dot(after(dkv, term, late), n_rows, ((0,), (0,))).astype(BF)
    early_terms = z_terms(early)
    late = sum_pair(z_terms(after(late, early_terms, d_pair)))
    early = sum_pair(early_terms)

    d_out = lax.psum_scatter(d_out, "y", scatter_dimension=0, tiled=True)
    d_pair = lax.psum_scatter(after(d_pair, d_out, early_terms), "y", scatter_dimension=0, tiled=True)
    late, term = after((late, term), d_pair)
    term = lax.psum_scatter(term, ROWS, scatter_dimension=0, tiled=True)
    d_query = reduce_ring([late[1], early[1], early[0], late[0]], "y")
    width = d_out.shape[1]
    d_pair = d_pair.reshape(4, -1, 2, ENC)
    rest = jnp.concatenate([d_out.reshape(4, -1, width), d_pair[:, :, 0], d_pair[:, :, 1]], 2)
    rest = sum_parts(after(rest, late).reshape(DH, -1), "z")
    d_query = z_gather(after(d_query, rest))
    rest = z_gather(rest)
    d_out = rest[:, :width]
    d_pair = jnp.stack([rest[:, width : width + ENC], rest[:, width + ENC :]], 1)
    d_pair = d_pair.reshape(2 * DH, ENC).T
    grad_tokens = unshift(term)
    return grad_tokens, d_query, d_pair[:, :DH], d_pair[:, DH:], d_out


def solution(mesh):
    devices = mesh.devices.reshape(4, 4, 4, 2)
    torus = Mesh(devices, ("z", "x", "y", "c"))
    rows = P(("z", "x", "y", "c"))
    cols = P(None, SEQ)
    in_specs = (rows, rows, rows, P(), P(), cols, cols, cols, P(SEQ))
    out_specs = (rows, cols, cols, cols, P(SEQ))
    return jax.shard_map(shards, mesh=torus, in_specs=in_specs, out_specs=out_specs, check_vma=False)
```
